128 devices in a mesh: seq: 16 (over y, x), fsdp: 8 (over z, core).
Axes of the slice: x: 4, y: 4, z: 4, core: 2. Of those that a mesh axis runs over, the one named last changes fastest.
Arguments:
- tokens: bfloat16 [8, 2048, 1024], P('fsdp', 'seq'), may hold values from -6 to 6
- cotangent: bfloat16 [8, 2048, 1024], P('fsdp', 'seq'), may hold values from -6 to 6
- segments: int32 [8, 2048], P('fsdp'), may hold values from 0 to 4, as said below
- pair_table: int32 [16], replicated, may hold values from 0 to 15, each once
- norm_gain: bfloat16 [1024], P('fsdp'), may hold values from 0.5 to 1.5
- w_query: bfloat16 [1024, 1024], P('fsdp'), may hold values from -0.1875 to 0.1875
- w_key: bfloat16 [1024, 512], P('fsdp'), may hold values from -0.1875 to 0.1875
- w_value: bfloat16 [1024, 512], P('fsdp'), may hold values from -0.1875 to 0.1875
- query_gain: bfloat16 [64], P('fsdp'), may hold values from 0.099609375 to 1.8984375
- key_gain: bfloat16 [64], P('fsdp'), may hold values from 0.099609375 to 1.8984375
- w_out: bfloat16 [1024, 1024], P('fsdp'), may hold values from -0.75 to 0.75
- ffn_gain: bfloat16 [1024], P('fsdp'), may hold values from 0.5 to 1.5
- w_gate: bfloat16 [1024, 4608], P('fsdp'), may hold values from -0.1875 to 0.1875
- w_up: bfloat16 [1024, 4608], P('fsdp'), may hold values from -0.1875 to 0.1875
- w_down: bfloat16 [4608, 1024], P('fsdp'), may hold values from -0.09375 to 0.09375
Outputs:
- block_out: bfloat16 [8, 2048, 1024], P('fsdp', 'seq')
- grad_tokens: bfloat16 [8, 2048, 1024], P('fsdp', 'seq')
- grad_norm_gain: float32 [1024], P('fsdp')
- grad_w_query: float32 [1024, 1024], P('fsdp')
- grad_w_key: float32 [1024, 512], P('fsdp')
- grad_w_value: float32 [1024, 512], P('fsdp')
- grad_query_gain: float32 [64], P('fsdp')
- grad_key_gain: float32 [64], P('fsdp')
- grad_w_out: float32 [1024, 1024], P('fsdp')
- grad_ffn_gain: float32 [1024], P('fsdp')
- grad_w_gate: float32 [1024, 4608], P('fsdp')
- grad_w_up: float32 [1024, 4608], P('fsdp')
- grad_w_down: float32 [4608, 1024], P('fsdp')
The draws below stay inside these ranges and needn't reach their ends.
Inputs may be any that keep to these rules, and one draw needn't show every extreme that they name: `segments`: segment ids never fall along a sequence; segment 0 covers at least the first half of every sequence. A permutation; device i of seq holds the blocks pair_table[i] and 31 - pair_table[i].
All inputs are finite; a program needn't handle non-finite values.
Results may differ from the reference program's by a relative error of at most 0.033.
Values may be sent and summed in bfloat16 or wider, within the bound.
No kernel may reach another device: no remote copies, remote signals or barrier semaphores. Data moves between devices by JAX's collectives and lax.ppermute only.
A program may use at most 192 MiB of HBM per device.

```python
import math
import jax
import jax.numpy as jnp
from jax import lax

D = 1024
H = 16
KVH = 8
HD = 64
FF = 4608
TOK_DEV = 128
SEQS = 8
LEN = 2048
N_SEQ = 16


def draw_segments(key, part):
    key = jax.random.fold_in(key, 11)
    first_key, other_key = jax.random.split(key)
    length = TOK_DEV * N_SEQ
    first_cut = jax.random.randint(first_key, (SEQS, 1), length // 2, length // 2 + length // 4 + 1)
    spread = jax.random.randint(other_key, (SEQS, 3), 0, length)
    other_cuts = first_cut + 1 + spread % (length - first_cut - 1)
    positions = jnp.arange(length, dtype=jnp.int32)[None, :]
    doc_ids = (positions >= first_cut).astype(jnp.int32)
    doc_ids = doc_ids + jnp.sum((positions[:, :, None] >= other_cuts[:, None, :]).astype(jnp.int32), axis=-1)
    return doc_ids.astype(jnp.int32)


def steps_of(own_key, extent, shards, smallest, largest):
    level, own = 1.0, jax.random.fold_in(own_key, 6)
    for position, blocks in shards:
        draws = jnp.exp(jax.random.uniform(jax.random.fold_in(own, position), (blocks,), jnp.float32, smallest / len(shards), largest / len(shards)))
        level = level * jnp.repeat(draws, extent[position] // blocks).reshape([-1 if axis == position else 1 for axis in range(len(extent))])
    return level


def bell_draw(own_key, extent, scale, most, cuts=(), kind=jnp.bfloat16):
    loudness = steps_of(own_key, extent, cuts, -0.22, 0.18) if cuts else 1.0
    drawn = jax.random.normal(own_key, extent, jnp.float32) * scale * loudness
    return jnp.minimum(jnp.maximum(drawn, -most), most).astype(kind)


def setup_inputs(seed: int = 0) -> dict:
    splits = jax.random.split(jax.random.key(seed), 16)
    tokens = bell_draw(splits[0], (SEQS, LEN, D), 1.0, 6.0, ((0, 8), (1, 16)))
    cotangent = bell_draw(splits[1], (SEQS, LEN, D), 1.0, 6.0, ((0, 8), (1, 16)))
    segments = draw_segments(jax.random.fold_in(splits[15], 71), 0)
    pair_table = jax.random.permutation(splits[3], N_SEQ).astype(jnp.int32)
    norm_gain = jnp.clip(1.0 + 0.1 * jax.random.normal(splits[4], (D,), jnp.float32), 0.5, 1.5).astype(jnp.bfloat16)
    w_query = bell_draw(splits[5], (D, H * HD), D ** -0.5, 0.1875, ((0, 8),))
    w_key = bell_draw(splits[6], (D, KVH * HD), D ** -0.5, 0.1875, ((0, 8),))
    w_value = bell_draw(splits[7], (D, KVH * HD), D ** -0.5, 0.1875, ((0, 8),))
    query_gain = jnp.clip(1.0 + 0.18 * jax.random.normal(splits[8], (HD,), jnp.float32), 0.099609375, 1.8984375).astype(jnp.bfloat16)
    key_gain = jnp.clip(1.0 + 0.18 * jax.random.normal(splits[9], (HD,), jnp.float32), 0.099609375, 1.8984375).astype(jnp.bfloat16)
    w_out = bell_draw(splits[10], (H * HD, D), HD ** -0.5, 0.75, ((0, 8),))
    ffn_gain = jnp.clip(1.0 + 0.1 * jax.random.normal(splits[11], (D,), jnp.float32), 0.5, 1.5).astype(jnp.bfloat16)
    w_gate = bell_draw(splits[12], (D, FF), D ** -0.5, 0.1875, ((0, 8),))
    w_up = bell_draw(splits[13], (D, FF), D ** -0.5, 0.1875, ((0, 8),))
    w_down = bell_draw(splits[14], (FF, D), FF ** -0.5, 0.09375, ((0, 8),))
    return dict(tokens=tokens, cotangent=cotangent, segments=segments, pair_table=pair_table, norm_gain=norm_gain, w_query=w_query, w_key=w_key, w_value=w_value, query_gain=query_gain, key_gain=key_gain, w_out=w_out, ffn_gain=ffn_gain, w_gate=w_gate, w_up=w_up, w_down=w_down)


epsilon = 1e-05
rope_base = 1000000.0
masked_value = -1e+30

@jax.custom_vjp
def low(v):
    return lax.optimization_barrier(v.astype(jnp.bfloat16)).astype(jnp.float32)

@jax.custom_vjp
def low_back(v):
    return v

def low_keep(v):
    return (low(v), None)

def low_pass(kept, grad):
    return (grad,)

def back_keep(v):
    return (v, None)

def back_low(kept, grad):
    return (low(grad),)
low.defvjp(low_keep, low_pass)
low_back.defvjp(back_keep, back_low)

def matmul(left_side, right_side):
    return jnp.dot(left_side, right_side, precision=lax.Precision.HIGHEST, preferred_element_type=jnp.float32)

def rms_scale(values):
    return lax.rsqrt(lax.optimization_barrier(jnp.mean(values * values, axis=-1, keepdims=True)) + epsilon)

def rotate(values, cosine, sine_table):
    half_width = values.shape[-1] // 2
    first_half = values[..., :half_width]
    second_half = values[..., half_width:]
    return jnp.concatenate([first_half * cosine - second_half * sine_table, second_half * cosine + first_half * sine_table], axis=-1)

def layout_positions(pair_table):
    half_rows = TOK_DEV // 2
    offsets = jnp.arange(half_rows, dtype=jnp.int32)
    early_start = pair_table * half_rows
    late_start = (2 * N_SEQ - 1 - pair_table) * half_rows
    both = jnp.concatenate([early_start[:, None] + offsets[None, :], late_start[:, None] + offsets[None, :]], axis=1)
    return both.reshape(TOK_DEV * N_SEQ).astype(jnp.int32)

def forward(inputs, params, cosine, sine_table, positions, doc_rows):
    gain_one, query_mat, key_mat, value_mat, gain_query, gain_key, out_mat, gain_two, gate_mat, up_mat, down_mat = params
    row_count = inputs.shape[0]
    group_size = H // KVH
    normed_one = low(inputs * rms_scale(inputs) * gain_one)
    query_raw = low_back(matmul(normed_one, query_mat)).reshape(row_count, H, HD)
    key_raw = low_back(matmul(normed_one, key_mat)).reshape(row_count, KVH, HD)
    value_low = low(low_back(matmul(normed_one, value_mat))).reshape(row_count, KVH, HD)
    query_low = low(rotate(query_raw * rms_scale(query_raw) * gain_query, cosine, sine_table))
    key_low = low(rotate(key_raw * rms_scale(key_raw) * gain_key, cosine, sine_table))
    block_rows = min(512, row_count)
    block_count = row_count // block_rows

    def attend(pieces):
        query_block, pos_block, doc_block = pieces
        scores = jnp.einsum('tkgd,jkd->kgtj', query_block, key_low, precision=lax.Precision.HIGHEST)
        scores = low_back(scores) * (1.0 / math.sqrt(HD))
        allowed = (positions[None, :] <= pos_block[:, None]) & (doc_rows[None, :] == doc_block[:, None])
        scores = jnp.where(allowed[None, None], scores, masked_value)
        row_peak = lax.optimization_barrier(jnp.max(scores, axis=-1, keepdims=True))
        exp_scores = jnp.exp(scores - row_peak)
        soft_weights = low(exp_scores / lax.optimization_barrier(jnp.sum(exp_scores, axis=-1, keepdims=True)))
        mixed_rows = jnp.einsum('kgtj,jkd->tkgd', soft_weights, value_low, precision=lax.Precision.HIGHEST)
        return mixed_rows.reshape(block_rows, H * HD)
    attended = lax.map(jax.checkpoint(attend), (query_low.reshape(block_count, block_rows, KVH, group_size, HD), positions.reshape(block_count, block_rows), doc_rows.reshape(block_count, block_rows)))
    attn_low = low(low_back(attended.reshape(row_count, H * HD)))
    hidden_one = inputs + low_back(matmul(attn_low, out_mat))
    normed_two = low(hidden_one * rms_scale(hidden_one) * gain_two)
    gate_val = low_back(matmul(normed_two, gate_mat))
    up_val = low_back(matmul(normed_two, up_mat))
    ffn_low = low(jax.nn.silu(gate_val) * up_val)
    return hidden_one + low_back(matmul(ffn_low, down_mat))

def reference(tokens, cotangent, segments, pair_table, norm_gain, w_query, w_key, w_value, query_gain, key_gain, w_out, ffn_gain, w_gate, w_up, w_down):
    positions = layout_positions(pair_table)
    exponents = jnp.arange(0, HD, 2).astype(jnp.float32) / HD
    angles = positions.astype(jnp.float32)[:, None] * (1.0 / rope_base ** exponents)[None, :]
    cosine = jnp.cos(angles)[:, None, :]
    sine_table = jnp.sin(angles)[:, None, :]
    params = tuple((w.astype(jnp.float32) for w in (norm_gain, w_query, w_key, w_value, query_gain, key_gain, w_out, ffn_gain, w_gate, w_up, w_down)))

    def one_sequence(totals, pieces):
        seq_in, seq_cot, seq_doc = pieces
        doc_rows = seq_doc[positions]

        def apply_layer(inputs, *weights_in):
            return forward(inputs, weights_in, cosine, sine_table, positions, doc_rows)
        layer_out, pull_back = jax.vjp(apply_layer, seq_in.astype(jnp.float32), *params)
        grads = pull_back(seq_cot.astype(jnp.float32))
        totals = tuple((a + b for a, b in zip(totals, grads[1:])))
        return (totals, (layer_out.astype(jnp.bfloat16), grads[0].astype(jnp.bfloat16)))
    zeros = tuple((jnp.zeros(w.shape, jnp.float32) for w in params))
    totals, outputs = lax.scan(one_sequence, zeros, (tokens, cotangent, segments))
    return (outputs[0], outputs[1], totals[0], totals[1], totals[2], totals[3], totals[4], totals[5], totals[6], totals[7], totals[8], totals[9], totals[10])
```

```python
import math

import jax
import jax.numpy as jnp
from jax import lax
from jax.experimental import pallas as pl
from jax.experimental.pallas import tpu as pltpu
from jax.sharding import PartitionSpec as P

EPS = 1e-05
ROPE_BASE = 1000000.0
F32 = jnp.float32
BF16 = jnp.bfloat16
BIG = 16384.0
LOG2E = 1.4426950408889634
LN2 = 0.6931471805599453
HD = 64
HALF = 64
TILE = 256
VMEM_LIMIT = 48 * 1024 * 1024


def dot_nt(a, b):
    return lax.dot_general(a, b, (((1,), (1,)), ((), ())), preferred_element_type=F32)


def dot_nn(a, b):
    return lax.dot_general(a, b, (((1,), (0,)), ((), ())), preferred_element_type=F32)


def dot_tn(a, b):
    return lax.dot_general(a, b, (((0,), (0,)), ((), ())), preferred_element_type=F32)


def lanes(shape):
    return lax.broadcasted_iota(jnp.int32, shape, 1)


def half_mean(t, lane):
    low = jnp.sum(jnp.where(lane < HD, t, 0.0), axis=-1, keepdims=True)
    high = jnp.sum(jnp.where(lane < HD, 0.0, t), axis=-1, keepdims=True)
    return jnp.where(lane < HD, low, high) * (1.0 / HD)


def partner(t, lane):
    return jnp.where((lane & (HD - 1)) < HD // 2, pltpu.roll(t, 96, 1), pltpu.roll(t, 32, 1))


def project_kernel(
    where_ref, xa, xb, xc, xd, w_ref, gain_ref, qk_gain_ref, cos_ref, sin_ref, doc_ref,
    n1_ref, raw_ref, q_ref, k_ref, v_ref,
):
    x = jnp.concatenate([xa[...], xb[...], xc[...], xd[...]], axis=0).astype(F32)
    scale = lax.rsqrt(jnp.mean(x * x, axis=-1, keepdims=True) + EPS)
    n1 = (x * scale * gain_ref[...]).astype(BF16)
    n1_ref[...] = n1
    y = dot_nn(n1, w_ref[...])
    raw = y[:, :128]
    raw_ref[...] = raw
    lane = lanes(raw.shape)
    normed = raw * lax.rsqrt(half_mean(raw * raw, lane) + EPS) * qk_gain_ref[...]
    turned = normed * cos_ref[...] + partner(normed, lane) * sin_ref[...]
    same = (lane - HD) == doc_ref[...]
    in_doc = (lane >= HD) & (lane < HD + 8)
    q_ref[...] = jnp.where(
        lane < HD, turned * (LOG2E / math.sqrt(HD)), jnp.where(same, 1.0, 0.0)
    ).astype(BF16)
    k_ref[...] = jnp.where(
        lane < HD, pltpu.roll(turned, 64, 1), jnp.where(in_doc & jnp.logical_not(same), -BIG, 0.0)
    ).astype(BF16)
    v_ref[...] = jnp.where(
        lane < HD, y[:, 128:], jnp.where(lane < HD + 2, 1.0, 0.0)
    ).astype(BF16)


def project(where, x_all, w, gain, qk_gain, cos, sin, doc):
    rows = x_all.shape[0]
    steps = rows // TILE

    def pick(j):
        return pl.BlockSpec((HALF, x_all.shape[1]), lambda g, t: (t[4 * g + j], 0))

    def whole(a):
        return pl.BlockSpec(a.shape, lambda g, t: (0, 0))

    def rowed(width):
        return pl.BlockSpec((TILE, width), lambda g, t: (g, 0))

    return pl.pallas_call(
        project_kernel,
        grid_spec=pltpu.PrefetchScalarGridSpec(
            num_scalar_prefetch=1,
            grid=(steps,),
            in_specs=[
                pick(0), pick(1), pick(2), pick(3),
                whole(w), whole(gain), whole(qk_gain),
                rowed(128), rowed(128), rowed(1),
            ],
            out_specs=[rowed(x_all.shape[1]), rowed(128), rowed(128), rowed(128), rowed(128)],
        ),
        out_shape=[
            jax.ShapeDtypeStruct((rows, x_all.shape[1]), BF16),
            jax.ShapeDtypeStruct((rows, 128), F32),
            jax.ShapeDtypeStruct((rows, 128), BF16),
            jax.ShapeDtypeStruct((rows, 128), BF16),
            jax.ShapeDtypeStruct((rows, 128), BF16),
        ],
        compiler_params=pltpu.CompilerParams(vmem_limit_bytes=VMEM_LIMIT),
        cost_estimate=pl.CostEstimate(
            flops=2 * rows * 1024 * 256, bytes_accessed=12 * 1024 * 1024, transcendentals=0
        ),
        name="project",
    )(where, x_all, x_all, x_all, x_all, w, gain, qk_gain, cos, sin, doc)


def forward_kernel(where_ref, q_ref, k_ref, v_ref, o_ref, kept_ref):
    rows = q_ref.shape[0]
    count = rows // TILE
    per = TILE // HALF
    half_blocks = rows // HALF // 2
    lower = lax.broadcasted_iota(jnp.int32, (TILE, TILE), 0) >= lax.broadcasted_iota(
        jnp.int32, (TILE, TILE), 1
    )
    lane = lanes((TILE, 128))
    for i in range(count):
        q = q_ref[i * TILE:(i + 1) * TILE, :]
        acc = jnp.zeros((TILE, 128), F32)
        for j in range(i + 1):
            e = jnp.exp2(dot_nt(q, k_ref[j * TILE:(j + 1) * TILE, :]))
            if j == i:
                e = jnp.where(lower, e, 0.0)
            acc = acc + dot_nn(e.astype(BF16), v_ref[j * TILE:(j + 1) * TILE, :])
        inverse = 1.0 / acc[:, HD:HD + 1]
        out = jnp.where(lane < HD, acc * inverse, inverse)
        kept_ref[i * TILE:(i + 1) * TILE, :] = out
        for b in range(per):
            block = i * per + b
            piece = out[b * HALF:(b + 1) * HALF, :HD].astype(BF16)
            slot = where_ref[block] // 2
            start = pl.multiple_of(slot * HALF, HALF)
            if block < half_blocks:
                o_ref[pl.ds(start, HALF), 0:HD] = piece
            else:
                o_ref[pl.ds(start, HALF), HD:2 * HD] = piece


def attend(where, q, k, v):
    rows = q.shape[0]
    vm = pl.BlockSpec(memory_space=pltpu.VMEM)
    return pl.pallas_call(
        forward_kernel,
        in_specs=[pl.BlockSpec(memory_space=pltpu.SMEM), vm, vm, vm],
        out_specs=[vm, vm],
        out_shape=[
            jax.ShapeDtypeStruct((rows // 2, 128), BF16),
            jax.ShapeDtypeStruct((rows, 128), F32),
        ],
        compiler_params=pltpu.CompilerParams(vmem_limit_bytes=VMEM_LIMIT),
        cost_estimate=pl.CostEstimate(
            flops=2 * rows * rows * 128, bytes_accessed=4 * 1024 * 1024, transcendentals=rows * rows // 2
        ),
        name="attend",
    )(where, q, k, v)


def backward_kernel(
    where_ref, q_ref, k_ref, v_ref, kept_ref, do_ref, raw_ref, cos_ref, sin_ref, gain_ref,
    grad_ref, packed_ref, gain_out_ref, dox, kt, dqt, dk_all, dv_all,
):
    rows = q_ref.shape[0]
    count = rows // TILE
    half_blocks = rows // HALF // 2
    lane64 = lanes((HALF, 128))
    for block in range(2 * half_blocks):
        start = pl.multiple_of((where_ref[block] // 2) * HALF, HALF)
        do = do_ref[pl.ds(start, HALF), :].astype(F32)
        if block >= half_blocks:
            do = pltpu.roll(do, 64, 1)
        kept = kept_ref[block * HALF:(block + 1) * HALF, :]
        inverse = kept[:, HD:HD + 1]
        scaled = do * inverse
        delta = jnp.sum(jnp.where(lane64 < HD, scaled * kept, 0.0), axis=-1, keepdims=True)
        top = delta.astype(BF16).astype(F32)
        dox[block * HALF:(block + 1) * HALF, :] = jnp.where(
            lane64 < HD,
            scaled,
            jnp.where(lane64 == HD, -top, jnp.where(lane64 == HD + 1, top - delta, 0.0)),
        ).astype(BF16)
    for j in range(count):
        kt[:, j * TILE:(j + 1) * TILE] = k_ref[j * TILE:(j + 1) * TILE, :].astype(F32).T.astype(BF16)
    upper = lax.broadcasted_iota(jnp.int32, (TILE, TILE), 0) <= lax.broadcasted_iota(
        jnp.int32, (TILE, TILE), 1
    )
    for j in range(count):
        key = k_ref[j * TILE:(j + 1) * TILE, :]
        value = v_ref[j * TILE:(j + 1) * TILE, :]
        key_turned = kt[:, j * TILE:(j + 1) * TILE]
        dk = jnp.zeros((TILE, 128), F32)
        dv = jnp.zeros((TILE, 128), F32)
        for i in range(j, count):
            span = slice(i * TILE, (i + 1) * TILE)
            q = q_ref[span, :]
            do = dox[span, :]
            e = jnp.exp2(dot_nt(key, q))
            if i == j:
                e = jnp.where(upper, e, 0.0)
            ds = (e * dot_nt(value, do)).astype(BF16)
            dv = dv + dot_nn(e.astype(BF16), do)
            dk = dk + dot_nn(ds, q)
            part = dot_nn(key_turned, ds)
            if j == 0:
                dqt[:, span] = part
            else:
                dqt[:, span] += part
        dk_all[j * TILE:(j + 1) * TILE, :] = dk
        dv_all[j * TILE:(j + 1) * TILE, :] = dv
    lane = lanes((TILE, 128))
    gain = gain_ref[...]
    gain_sum = jnp.zeros((1, 128), F32)
    per = TILE // HALF
    for i in range(count):
        span = slice(i * TILE, (i + 1) * TILE)
        dq = dqt[:, span].T
        both = jnp.where(
            lane < HD, dq * (1.0 / math.sqrt(HD)), pltpu.roll(dk_all[span, :], 64, 1) * LN2
        )
        dz = both * cos_ref[span, :] - partner(both, lane) * sin_ref[span, :]
        raw = raw_ref[span, :]
        scale = lax.rsqrt(half_mean(raw * raw, lane) + EPS)
        u = dz * gain
        back = scale * u - raw * scale * scale * scale * half_mean(u * raw, lane)
        gain_sum = gain_sum + jnp.sum(dz * raw * scale, axis=0, keepdims=True)
        back = back.astype(BF16)
        dv = dv_all[span, :]
        grad_ref[span, 0:128] = back
        grad_ref[span, 128:256] = jnp.where(lane < HD, dv, 0.0).astype(BF16)
        for b in range(per):
            block = i * per + b
            sub = slice(b * HALF, (b + 1) * HALF)
            start = pl.multiple_of((where_ref[block] // 2) * HALF, HALF)
            if block < half_blocks:
                packed_ref[pl.ds(start, HALF), 0:128] = back[sub]
                packed_ref[pl.ds(start, HALF), 256:256 + HD] = dv[sub, :HD].astype(BF16)
            else:
                packed_ref[pl.ds(start, HALF), 128:256] = back[sub]
                packed_ref[pl.ds(start, HALF), 256 + HD:384] = dv[sub, :HD].astype(BF16)
    gain_out_ref[...] = jnp.broadcast_to(gain_sum, (8, 128))


def attend_back(where, q, k, v, kept, do, raw, cos, sin, gain):
    rows = q.shape[0]
    vm = pl.BlockSpec(memory_space=pltpu.VMEM)
    return pl.pallas_call(
        backward_kernel,
        in_specs=[pl.BlockSpec(memory_space=pltpu.SMEM)] + [vm] * 9,
        out_specs=[vm, vm, vm],
        out_shape=[
            jax.ShapeDtypeStruct((rows, 256), BF16),
            jax.ShapeDtypeStruct((rows // 2, 384), BF16),
            jax.ShapeDtypeStruct((8, 128), F32),
        ],
        scratch_shapes=[
            pltpu.VMEM((rows, 128), BF16),
            pltpu.VMEM((128, rows), BF16),
            pltpu.VMEM((128, rows), F32),
            pltpu.VMEM((rows, 128), F32),
            pltpu.VMEM((rows, 128), F32),
        ],
        compiler_params=pltpu.CompilerParams(vmem_limit_bytes=VMEM_LIMIT),
        cost_estimate=pl.CostEstimate(
            flops=5 * rows * rows * 128, bytes_accessed=8 * 1024 * 1024, transcendentals=rows * rows // 2
        ),
        name="attend_back",
    )(where, q, k, v, kept, do, raw, cos, sin, gain)


def swap(a, axis):
    return lax.all_to_all(a, axis, split_axis=0, concat_axis=0, tiled=True)


def spread(a, axis):
    count = lax.axis_size(axis)
    return swap(jnp.broadcast_to(a[None], (count,) + a.shape), axis)


def sum_parts(a):
    return jnp.sum(a.astype(F32), axis=0)


def after(value, *others):
    return lax.optimization_barrier((value,) + others)[0]


def scale_of(v):
    return lax.rsqrt(jnp.mean(v * v, axis=-1, keepdims=True) + EPS)


def norm_back(values, scaling, gain, incoming):
    weighted = incoming * gain
    inner = jnp.mean(weighted * values, axis=-1, keepdims=True)
    return scaling * weighted - values * scaling * scaling * scaling * inner


def body(
    tokens, cotangent, segments, pair_table, norm_gain, w_query, w_key, w_value,
    query_gain, key_gain, w_out, ffn_gain, w_gate, w_up, w_down,
):
    n_seq = lax.axis_size("seq")
    n_f = lax.axis_size("fsdp")
    me = lax.axis_index("seq")
    toks, width = tokens.shape[1:]
    rows = toks * n_seq
    own_rows = w_query.shape[0]
    kv_width = w_key.shape[1]
    kv_heads = kv_width // HD
    ff = w_gate.shape[1]
    ff_own = ff // n_f

    x_all = lax.all_gather(tokens[0], "seq", axis=0, tiled=True)

    slots = jnp.arange(n_seq, dtype=jnp.int32)
    blocks = jnp.arange(n_seq, dtype=jnp.int32)
    slot_of = jnp.sum(
        jnp.where(pair_table[None, :] == blocks[:, None], slots[None, :], 0), axis=1
    ).astype(jnp.int32)
    where = jnp.concatenate([2 * slot_of, 2 * slot_of[::-1] + 1])

    exponents = jnp.arange(0, HD, 2).astype(F32) / HD
    angles = jnp.arange(rows, dtype=F32)[:, None] * (1.0 / ROPE_BASE**exponents)[None, :]
    cosine, sine = jnp.cos(angles), jnp.sin(angles)
    cos = jnp.concatenate([cosine, cosine, cosine, cosine], axis=1)
    sin = jnp.concatenate([-sine, sine, -sine, sine], axis=1)
    doc = segments[0][:, None]

    gain_cols = jnp.concatenate(
        [
            norm_gain[:, None],
            ffn_gain[:, None],
            jnp.pad(query_gain, (0, own_rows - query_gain.shape[0]))[:, None],
            jnp.pad(key_gain, (0, own_rows - key_gain.shape[0]))[:, None],
            jnp.zeros((own_rows, 60), BF16),
        ],
        axis=1,
    )
    pair = me // 2
    own_slice = jnp.concatenate(
        [
            lax.dynamic_slice_in_dim(w_query, me * HD, HD, 1),
            lax.dynamic_slice_in_dim(w_key, pair * HD, HD, 1),
            lax.dynamic_slice_in_dim(w_value, pair * HD, HD, 1),
            gain_cols,
        ],
        axis=1,
    )
    w_head = spread(own_slice, "fsdp")
    gain_one = w_head[:, :, 192].reshape(1, width).astype(F32)
    gain_two = w_head[:, :, 193].reshape(1, width).astype(F32)
    q_gain = w_head[:, : HD // n_f, 194].reshape(1, HD).astype(F32)
    k_gain = w_head[:, : HD // n_f, 195].reshape(1, HD).astype(F32)
    qk_gain = jnp.concatenate([q_gain, k_gain], axis=1)
    w_head = w_head.reshape(width, 256)

    def to_columns(w):
        return swap(w.reshape(own_rows, n_f, ff_own).transpose(1, 0, 2), "fsdp").reshape(
            width, ff_own
        )

    gate_mat = to_columns(w_gate)
    up_mat = to_columns(w_up)

    n1_all, raw, q, k, v = project(where, x_all, w_head, gain_one, qk_gain, cos, sin, doc)
    both = after(jnp.concatenate([w_out, cotangent[0]], axis=0), x_all)
    both_all = lax.all_gather(both, "fsdp", axis=0, tiled=True).reshape(n_f, -1, width)
    out_mat = both_all[:, :own_rows].reshape(width, width)
    g_all = both_all[:, own_rows:].reshape(n_f * toks, width)

    o_packed, kept = attend(where, q, k, v)

    def to_tokens(a):
        return a.reshape(n_seq, HALF, 2, HD).transpose(2, 1, 0, 3).reshape(toks, n_seq * HD)

    def to_heads(a):
        return a.reshape(2, HALF, n_seq, HD).transpose(2, 1, 0, 3).reshape(n_seq, HALF, 2 * HD)

    o_tok = to_tokens(swap(o_packed.reshape(n_seq, HALF, 128), "seq"))
    x = tokens[0].astype(F32)
    h1 = x + dot_nn(o_tok, out_mat)
    scale_two = scale_of(h1)
    n2 = (h1 * scale_two * gain_two).astype(BF16)
    n2_all = lax.all_gather(n2, "fsdp", axis=0, tiled=True)

    qkv_local = after(jnp.concatenate([w_query, w_key, w_value], axis=1), n2_all)
    qkv_mat = lax.all_gather(qkv_local, "fsdp", axis=0, tiled=True)

    gate = dot_nn(n2_all, gate_mat)
    up = dot_nn(n2_all, up_mat)
    sig = jax.nn.sigmoid(gate)
    f_low = (gate * sig * up).astype(BF16)
    df = dot_nt(g_all, w_down)
    dup = (df * gate * sig).astype(BF16)
    dgate = (df * up * sig * (1.0 + gate * (1.0 - sig))).astype(BF16)
    dn2_part = (dot_nt(dgate, gate_mat) + dot_nt(dup, up_mat)).astype(BF16)
    dn2 = sum_parts(swap(dn2_part.reshape(n_f, toks, width), "fsdp"))

    grad_down_part = dot_tn(f_low, g_all).astype(BF16)
    grad_gate_part = dot_tn(n2_all, dgate).astype(BF16)
    grad_up_part = dot_tn(n2_all, dup).astype(BF16)
    down_part = dot_nn(f_low, w_down).astype(BF16)
    down = lax.psum_scatter(down_part, "fsdp", scatter_dimension=0, tiled=True)
    block_out = (h1 + down.astype(F32)).astype(BF16)

    g = cotangent[0].astype(F32)
    dh1 = g + norm_back(h1, scale_two, gain_two, dn2)
    dh = dh1.astype(BF16)
    do = dot_nt(dh, out_mat).astype(BF16)
    do_packed = swap(to_heads(do), "seq").reshape(rows // 2, 128)
    grad_out_part = dot_tn(o_tok, dh).astype(BF16)

    grad_head, packed, gain_part = attend_back(
        where, q, k, v, kept, do_packed, raw, cos, sin, qk_gain
    )

    own_share = own_rows // n_seq
    down_share = ff_own // n_seq

    def by_seq(a):
        return (
            a.reshape(n_f, n_seq, own_share, ff_own)
            .transpose(1, 0, 2, 3)
            .reshape(n_seq, n_f * own_share, ff_own)
        )

    down_sum = sum_parts(swap(grad_down_part.reshape(n_seq, down_share, width), "seq")).astype(BF16)
    gu_sum = sum_parts(
        swap(jnp.concatenate([by_seq(grad_gate_part), by_seq(grad_up_part)], axis=1), "seq")
    ).astype(BF16)
    gu_rows = swap(
        gu_sum.reshape(2, n_f, own_share, ff_own)
        .transpose(1, 0, 2, 3)
        .reshape(n_f, 2 * own_share, ff_own),
        "fsdp",
    )
    gu_rows = gu_rows.transpose(1, 0, 2).reshape(2, own_share, ff // 512, 512)
    gu_rows = gu_rows.transpose(0, 2, 1, 3).reshape(2 * own_share * (ff // 512), 512)
    down_pad = -down_share % 8
    down_rows = jnp.pad(down_sum, ((0, down_pad), (0, 0)))
    down_rows = jnp.concatenate([down_rows[:, :512], down_rows[:, 512:]], axis=0)
    gu_count = gu_rows.shape[0]
    ffn_all = lax.all_gather(
        jnp.concatenate([gu_rows, down_rows], axis=0), "seq", axis=0, tiled=True
    ).reshape(n_seq, -1, 512)
    gu_all = (
        ffn_all[:, :gu_count]
        .reshape(n_seq, 2, ff // 512, own_share, 512)
        .transpose(1, 0, 3, 2, 4)
        .reshape(2, own_rows, ff)
    )
    grad_gate = gu_all[0].astype(F32)
    grad_up = gu_all[1].astype(F32)
    down_all = ffn_all[:, gu_count:].reshape(n_seq, 2, down_share + down_pad, 512)[:, :, :down_share]
    grad_down = down_all.transpose(0, 2, 1, 3).reshape(ff_own, width).astype(F32)

    out_rows = sum_parts(swap(grad_out_part.reshape(n_f, own_rows, width), "fsdp")).astype(BF16)
    out_rows = sum_parts(swap(out_rows.reshape(n_seq, own_share, width), "seq")).astype(BF16)
    head_part = dot_tn(n1_all, grad_head[:, :192]).astype(BF16)
    gain_part = gain_part[0].reshape(2, n_f, HD // n_f).transpose(1, 0, 2).reshape(n_f, 1, 2 * HD // n_f)
    gain_part = jnp.pad(
        gain_part.astype(BF16), ((0, 0), (0, own_rows - 1), (0, HD - gain_part.shape[2]))
    )
    head_part = jnp.concatenate([head_part.reshape(n_f, own_rows, 192), gain_part], axis=2)
    head_sum = sum_parts(swap(head_part, "fsdp")).astype(BF16)
    last = jnp.concatenate(
        [head_sum, out_rows.reshape(own_share, width // 256, 256).transpose(1, 0, 2).reshape(-1, 256)],
        axis=0,
    )
    last_all = spread(last, "seq").astype(F32)
    heads_all = last_all[:, :own_rows]
    grad_query = heads_all[:, :, :HD].transpose(1, 0, 2).reshape(own_rows, n_seq * HD)

    def pair_sum(a):
        return (
            a.reshape(kv_heads, 2, own_rows, HD)
            .sum(axis=1)
            .transpose(1, 0, 2)
            .reshape(own_rows, kv_width)
        )

    grad_key = pair_sum(heads_all[:, :, HD:2 * HD])
    grad_value = pair_sum(heads_all[:, :, 2 * HD:3 * HD])
    gain_all = jnp.sum(heads_all[:, 0, 192:192 + 2 * HD // n_f], axis=0)
    grad_query_gain = gain_all[: HD // n_f]
    grad_key_gain = gain_all[HD // n_f:]
    grad_out = (
        last_all[:, own_rows:]
        .reshape(n_seq, width // 256, own_share, 256)
        .transpose(0, 2, 1, 3)
        .reshape(own_rows, width)
    )

    def dots(w, grad):
        return jnp.sum(w.astype(F32) * grad, axis=1)

    grad_norm_gain = (
        dots(w_query, grad_query) + dots(w_key, grad_key) + dots(w_value, grad_value)
    ) / norm_gain.astype(F32)
    grad_ffn_gain = (dots(w_gate, grad_gate) + dots(w_up, grad_up)) / ffn_gain.astype(F32)

    arrived = swap(packed.reshape(n_seq, HALF, 384), "seq")
    qk_tok = arrived[:, :, :256].reshape(n_seq, HALF, 2, 2, HD)
    dq_tok = qk_tok[:, :, :, 0].transpose(2, 1, 0, 3).reshape(toks, n_seq * HD)

    def pair_tokens(a):
        a = a.astype(F32).reshape(kv_heads, 2, HALF, 2, HD).sum(axis=1)
        return a.transpose(2, 1, 0, 3).reshape(toks, kv_width).astype(BF16)

    dk_tok = pair_tokens(qk_tok[:, :, :, 1])
    dv_tok = pair_tokens(arrived[:, :, 256:].reshape(n_seq, HALF, 2, HD))
    dn1 = dot_nt(jnp.concatenate([dq_tok, dk_tok, dv_tok], axis=1), qkv_mat)
    grad_tokens = (dh1 + norm_back(x, scale_of(x), gain_one, dn1)).astype(BF16)

    return (
        block_out[None],
        grad_tokens[None],
        grad_norm_gain,
        grad_query,
        grad_key,
        grad_value,
        grad_query_gain,
        grad_key_gain,
        grad_out,
        grad_ffn_gain,
        grad_gate,
        grad_up,
        grad_down,
    )


def solution(mesh):
    row = P("fsdp", None)
    vec = P("fsdp")
    tok = P("fsdp", "seq", None)
    return jax.shard_map(
        body,
        mesh=mesh,
        in_specs=(
            tok, tok, row, P(), vec, row, row, row, vec, vec, row, vec, row, row, row,
        ),
        out_specs=(
            tok, tok, vec, row, row, row, vec, vec, row, vec, row, row, row,
        ),
        check_vma=False,
    )
```

```python
import math

import jax
import jax.numpy as jnp
import numpy as np
from jax import lax
from jax.experimental import pallas as pl
from jax.experimental.pallas import tpu as pltpu
from jax.sharding import PartitionSpec as P

EPS = 1e-05
ROPE_BASE = 1000000.0
F32 = jnp.float32
BF16 = jnp.bfloat16
BIG = 16384.0
LOG2E = 1.4426950408889634
LN2 = 0.6931471805599453
HD = 64
HALF = 64
TILE = 256
VMEM_LIMIT = 52 * 1024 * 1024
UNITS = 5


def dot_nt(a, b):
    return lax.dot_general(a, b, (((1,), (1,)), ((), ())), preferred_element_type=F32)


def dot_nn(a, b):
    return lax.dot_general(a, b, (((1,), (0,)), ((), ())), preferred_element_type=F32)


def dot_tn(a, b):
    return lax.dot_general(a, b, (((0,), (0,)), ((), ())), preferred_element_type=F32)


def lanes(shape):
    return lax.broadcasted_iota(jnp.int32, shape, 1)


def half_mean(t, lane):
    low = jnp.sum(jnp.where(lane < HD, t, 0.0), axis=-1, keepdims=True)
    high = jnp.sum(jnp.where(lane < HD, 0.0, t), axis=-1, keepdims=True)
    return jnp.where(lane < HD, low, high) * (1.0 / HD)


def partner(t, lane):
    return jnp.where((lane & (HD - 1)) < HD // 2, pltpu.roll(t, 96, 1), pltpu.roll(t, 32, 1))


def vmem(count):
    return [pl.BlockSpec(memory_space=pltpu.VMEM)] * count


SMEM = pl.BlockSpec(memory_space=pltpu.SMEM)


def shape(dims, kind):
    return jax.ShapeDtypeStruct(dims, kind)


def part_of(block, *at):
    return pl.BlockSpec(block, lambda i: at)


def call(kernel, name, ins, outs, out_shape, scratch, flops, size, *args):
    return pl.pallas_call(
        kernel,
        grid=(1,),
        in_specs=ins,
        out_specs=outs,
        out_shape=out_shape,
        scratch_shapes=scratch,
        compiler_params=pltpu.CompilerParams(vmem_limit_bytes=VMEM_LIMIT),
        cost_estimate=pl.CostEstimate(flops=flops, bytes_accessed=size, transcendentals=0),
        name=name,
    )(*args)


def pack_kernel(
    spot_ref, qg_ref, kg_ref, gains_ref, wq_ref, wk_ref, wv_ref, wg_ref, wu_ref, wo_ref, g_ref,
    out_ref, both_ref,
):
    n_f, own, _ = out_ref.shape
    ff_own = wg_ref.shape[1] // n_f
    both_ref[0:own, :] = wo_ref[...]
    both_ref[own:, :] = g_ref[...]
    me = spot_ref[0]
    mine = spot_ref[1]
    lane = lanes((own, 128))
    pair = me // 2

    def tile(ref, head):
        at = pl.multiple_of((head // 2) * 128, 128)
        t = ref[:, pl.ds(at, 128)].astype(F32)
        odd = jnp.broadcast_to(lax.rem(head, 2), t.shape) == 1
        turned = pltpu.roll(t, 64, 1)
        return jnp.where(odd, turned, t), jnp.where(odd, t, turned)

    q = tile(wq_ref, me)[0]
    k = tile(wk_ref, pair)[1]
    v = tile(wv_ref, pair)[0]
    gains = jnp.concatenate([gains_ref[...], jnp.zeros((120, 128), F32)], axis=0).T
    second = jnp.where(lane < HD, v, pltpu.roll(gains, 64, 1))
    row = lax.broadcasted_iota(jnp.int32, (8, 128), 0)
    lane8 = lanes((8, 128))
    group = mine // 4
    at = 96 + 8 * lax.rem(mine, 4)
    extra = jnp.zeros((8, 128), F32)
    for j in range(qg_ref.shape[0]):
        extra = jnp.where((lane8 == at + j) & (row == group), qg_ref[j], extra)
        extra = jnp.where((lane8 == at + j) & (row == group + 2), kg_ref[j], extra)
    second = jnp.concatenate([second[0:8] + extra, second[8:]], axis=0).astype(BF16)
    first = jnp.where(lane < HD, q, k).astype(BF16)
    for c in range(n_f):
        out_ref[c, :, 0:128] = first
        out_ref[c, :, 128:256] = second
        out_ref[c, :, 256:256 + ff_own] = wg_ref[:, c * ff_own:(c + 1) * ff_own]
        out_ref[c, :, 256 + ff_own:256 + 2 * ff_own] = wu_ref[:, c * ff_own:(c + 1) * ff_own]


def pack_weights(spot, qg, kg, gains, wq, wk, wv, wg, wu, wo, g, n_f):
    own, width = wq.shape
    return call(
        pack_kernel, "pack_weights", [SMEM] * 3 + vmem(8), vmem(2),
        [
            shape((n_f, own, 256 + 2 * wg.shape[1] // n_f), BF16),
            shape((own + g.shape[0], width), BF16),
        ],
        [], 1024, 6 * 1024 * 1024,
        spot, qg, kg, gains, wq, wk, wv, wg, wu, wo, g,
    )


def home_of(spot_ref, step, other, count):
    mine = spot_ref[1]
    core = lax.rem(mine, 2)
    return lax.rem(mine - core - 2 * step + count, count) + (1 - core if other else core)


def forward_kernel(
    where_ref, x_ref, w_ref, cos_ref, sin_ref, doc_ref,
    o_ref, kept_ref, raw_ref, scale_ref, q_ref, k_ref, v_ref, gains_ref, qk_gain_ref,
):
    rows = x_ref.shape[0]
    count = rows // TILE
    per = TILE // HALF
    half_blocks = rows // HALF // 2
    w = w_ref[...].astype(F32)
    gains_ref[...] = w[:, 128:].T[HD:HD + 8]
    found = jnp.zeros((8, 128), F32)
    for c in range(w.shape[0] // 128):
        found = found + w[c * 128:c * 128 + 8, 128:]
    lane8 = lanes((8, 128))
    qk_gain = jnp.zeros((8, 128), F32)
    for part in range(4):
        line = jnp.broadcast_to(found[part:part + 1], (8, 128))
        if part < 3:
            line = pltpu.roll(line, 32 * (part + 1), 1)
        qk_gain = jnp.where(lane8 // 32 == part, line, qk_gain)
    qk_gain_ref[...] = qk_gain
    qk_gain = qk_gain[0:1]
    w = (w * w[:, 192:193]).astype(BF16)
    lane = lanes((TILE, 128))
    docs = doc_ref[...]
    docs = jnp.concatenate([docs, jnp.zeros((128 - docs.shape[0], 128), F32)], axis=0).T
    spread_lane = (lane - HD).astype(F32)
    for i in range(count):
        span = slice(i * TILE, (i + 1) * TILE)
        pieces = []
        for b in range(per):
            start = pl.multiple_of(where_ref[i * per + b] * HALF, HALF)
            pieces.append(x_ref[pl.ds(start, HALF), :])
        x_low = jnp.concatenate(pieces, axis=0)
        x = x_low.astype(F32)
        scale = lax.rsqrt(jnp.mean(x * x, axis=-1, keepdims=True) + EPS)
        y = dot_nn(x_low, w) * scale
        scale_ref[span, :] = jnp.broadcast_to(scale, (TILE, 128))
        raw = y[:, :128]
        raw_ref[span, :] = raw
        normed = raw * lax.rsqrt(half_mean(raw * raw, lane) + EPS) * qk_gain
        turned = normed * cos_ref[span, :] + partner(normed, lane) * sin_ref[span, :]
        doc = jnp.concatenate([docs[:, 2 * i:2 * i + 1], docs[:, 2 * i + 1:2 * i + 2]], axis=0)
        mark = jnp.where(spread_lane == doc, 1.0, 0.0)
        q_ref[span, :] = jnp.where(
            lane < HD, turned * (LOG2E / math.sqrt(HD)), mark
        ).astype(BF16)
        k_ref[span, :] = jnp.where(
            lane < HD,
            pltpu.roll(turned, 64, 1),
            jnp.where(lane < HD + 8, (mark - 1.0) * BIG, 0.0),
        ).astype(BF16)
        v_ref[span, :] = jnp.where(
            lane < HD, y[:, 128:], jnp.where(lane < HD + 2, 1.0, 0.0)
        ).astype(BF16)
    lower = lax.broadcasted_iota(jnp.int32, (TILE, TILE), 0) >= lax.broadcasted_iota(
        jnp.int32, (TILE, TILE), 1
    )
    for i in range(count):
        q = q_ref[i * TILE:(i + 1) * TILE, :]
        acc = jnp.zeros((TILE, 128), F32)
        for j in range(i + 1):
            e = jnp.exp2(dot_nt(q, k_ref[j * TILE:(j + 1) * TILE, :]))
            if j == i:
                e = jnp.where(lower, e, 0.0)
            acc = acc + dot_nn(e.astype(BF16), v_ref[j * TILE:(j + 1) * TILE, :])
        inverse = 1.0 / acc[:, HD:HD + 1]
        out = jnp.where(lane < HD, acc * inverse, inverse)
        kept_ref[i * TILE:(i + 1) * TILE, :] = out
        for b in range(per):
            block = i * per + b
            piece = out[b * HALF:(b + 1) * HALF, :HD].astype(BF16)
            start = pl.multiple_of((where_ref[block] // 2) * HALF, HALF)
            if block < half_blocks:
                o_ref[pl.ds(start, HALF), 0:HD] = piece
            else:
                o_ref[pl.ds(start, HALF), HD:2 * HD] = piece


def attend(where, x_all, w, cos, sin, doc):
    rows, width = x_all.shape
    return call(
        forward_kernel, "attend", [SMEM] + vmem(1) + [part_of((width, 256), 0, 0)] + vmem(3), vmem(9),
        [
            shape((rows // 2, 128), BF16),
            shape((rows, 128), F32),
            shape((rows, 128), F32),
            shape((rows, 128), F32),
            shape((rows, 128), BF16),
            shape((rows, 128), BF16),
            shape((rows, 128), BF16),
            shape((8, w.shape[0]), F32),
            shape((8, 128), F32),
        ],
        [], 3 * rows * rows * 128, 10 * 1024 * 1024,
        where, x_all, w, cos, sin, doc,
    )


def unfold(o_ref, target, heads):
    for pair in range(heads // 2):
        a = o_ref[2 * pair].astype(F32)
        b = o_ref[2 * pair + 1].astype(F32)
        lane = lanes(a.shape)
        span = slice(pair * 128, (pair + 1) * 128)
        target[0:HALF, span] = jnp.where(lane < HD, a, pltpu.roll(b, 64, 1)).astype(BF16)
        target[HALF:2 * HALF, span] = jnp.where(lane < HD, pltpu.roll(a, 64, 1), b).astype(BF16)


def out_kernel(o_ref, mat_ref, x_ref, gain_ref, h_ref, n_ref, chunk_ref, o_tok):
    heads = o_ref.shape[0]
    unfold(o_ref, o_tok, heads)
    for c in range(heads // 2):
        chunk_ref[c] = o_tok[:, c * 128:(c + 1) * 128]
    h = x_ref[...].astype(F32) + dot_nn(o_tok[...], mat_ref[...].reshape(-1, x_ref.shape[1]))
    h_ref[...] = h
    scale = lax.rsqrt(jnp.mean(h * h, axis=-1, keepdims=True) + EPS)
    n_ref[...] = (h * scale * gain_ref[1:2, :]).astype(BF16)


def project_out(o, mat, x, gain):
    toks, width = x.shape
    return call(
        out_kernel, "project_out",
        vmem(1) + [part_of((width // 128, 128, width), 0, 0, 0)] + vmem(2), vmem(3),
        [
            shape((toks, width), F32),
            shape((toks, width), BF16),
            shape((width // 128, toks, 128), BF16),
        ],
        [pltpu.VMEM((toks, width), BF16)], 2 * toks * width * width, 3 * 1024 * 1024,
        o, mat, x, gain,
    )


def turn(a):
    return a.astype(F32).T.astype(BF16)


def prepare_kernel(
    w_ref, down_ref, both_ref, gate_ref, up_ref, gate_t_ref, up_t_ref, down_t_ref, out_t_ref
):
    own = gate_ref.shape[1]
    rows = both_ref.shape[1]
    for c in range(w_ref.shape[0] // rows):
        span = slice(c * rows, (c + 1) * rows)
        gate = w_ref[span, 256:256 + own]
        up = w_ref[span, 256 + own:256 + 2 * own]
        gate_ref[span, :] = gate
        up_ref[span, :] = up
        gate_t_ref[:, span] = turn(gate)
        up_t_ref[:, span] = turn(up)
        down_t_ref[span, :] = turn(down_ref[:, span])
        out_t_ref[:, span] = turn(both_ref[c])


def prepare(w_big, down_mat, both):
    own, width = down_mat.shape
    tall, wide = shape((width, own), BF16), shape((own, width), BF16)
    return call(
        prepare_kernel, "prepare",
        vmem(2) + [part_of((both.shape[0], both.shape[1] // 2, width), 0, 0, 0)], vmem(6),
        [tall, tall, wide, wide, tall, shape((width, width), BF16)],
        [], 1024, 16 * 1024 * 1024,
        w_big, down_mat, both,
    )


def ffn_kernel(
    n_ref, g_ref, gate_mat, up_mat, gate_t, up_t, down_t, part_ref, f_ref, dgate_ref, dup_ref
):
    g = g_ref[...].reshape(-1, n_ref.shape[1])
    n = n_ref[...]
    gate = dot_nn(n, gate_mat[...])
    up = dot_nn(n, up_mat[...])
    df = dot_nn(g, down_t[...])
    sig = jax.nn.sigmoid(gate)
    act = gate * sig
    f_ref[...] = (act * up).astype(BF16)
    dup = (df * act).astype(BF16)
    dgate = (df * up * sig * (1.0 + gate * (1.0 - sig))).astype(BF16)
    dup_ref[...] = dup
    dgate_ref[...] = dgate
    part = dot_nn(dgate, gate_t[...]) + dot_nn(dup, up_t[...])
    part_ref[...] = part.astype(BF16).reshape(part_ref.shape)


def ffn(n2, both, mats):
    rows, width = n2.shape
    own = mats[0].shape[1]
    n_f = both.shape[0]
    toks = rows // n_f
    group = n_f // 2
    block = group * toks

    def rowed(cols):
        return pl.BlockSpec((block, cols), lambda i: (i, 0))

    def whole(a):
        return pl.BlockSpec(a.shape, lambda i: (0, 0))

    return pl.pallas_call(
        ffn_kernel,
        grid=(n_f // group,),
        in_specs=[
            rowed(width),
            pl.BlockSpec((group, toks, width), lambda i: (i, 1, 0)),
        ] + [whole(m) for m in mats],
        out_specs=[
            pl.BlockSpec((group, toks, width), lambda i: (i, 0, 0)),
            rowed(own), rowed(own), rowed(own),
        ],
        out_shape=[
            shape((n_f, toks, width), BF16),
            shape((rows, own), BF16),
            shape((rows, own), BF16),
            shape((rows, own), BF16),
        ],
        compiler_params=pltpu.CompilerParams(vmem_limit_bytes=VMEM_LIMIT),
        cost_estimate=pl.CostEstimate(
            flops=10 * rows * width * own, bytes_accessed=16 * 1024 * 1024, transcendentals=rows * own
        ),
        name="ffn",
    )(n2, both, *mats)


def ffn_grads_kernel(
    spot_ref, place_ref, n_ref, g_ref, f_ref, dgate_ref, dup_ref, down_ref, *refs
):
    n_f = n_ref.shape[1] // 128
    own = f_ref.shape[1]
    side = refs[0].shape[0]
    one, two = refs[:side], refs[side:2 * side]
    keep_ref, give_ref, gu, dn = refs[2 * side:]
    cut = refs[0].shape[1]
    dgate = dgate_ref[...]
    dup = dup_ref[...]
    gu[:, own:640] = jnp.zeros((256, 640 - own), F32)

    def put(dy, dx, at, unit):
        unit = unit.astype(BF16)
        size = unit.shape[0]
        first = min(size, max(0, cut - at))
        if first > 0:
            one[dx][dy, at:at + first, :] = unit[:first]
        if first < size:
            lo = at + first - cut
            two[dy][dx, lo:lo + size - first, :] = unit[first:]

    for c in range(n_f):
        lhs = n_ref[:, c * 128:(c + 1) * 128]
        gu[0:128, 0:own] = dot_tn(lhs, dgate)
        gu[128:256, 0:own] = dot_tn(lhs, dup)
        for dy in range(side):
            for dx in range(side):
                s = place_ref[side * dy + dx]
                start = pl.multiple_of(8 * s, 8)
                gate = gu[pl.ds(start, 8), :]
                up = gu[pl.ds(pl.multiple_of(128 + start, 8), 8), :]
                for k in range(UNITS):
                    unit = jnp.concatenate(
                        [gate[:, 128 * k:128 * (k + 1)], up[:, 128 * k:128 * (k + 1)]], axis=0
                    )
                    put(dy, dx, (c * UNITS + k) * 16, unit)
    g = g_ref[...].reshape(-1, n_ref.shape[1])
    for c in range((own + 127) // 128):
        lo = 128 * c
        hi = min(own, lo + 128)
        dn[lo:hi, :] = dot_tn(f_ref[:, lo:hi], g)
    base = n_f * UNITS * 16
    tall = own // 8
    half = g.shape[1] // 2
    for dy in range(side):
        for dx in range(side):
            s = place_ref[side * dy + dx]
            start = pl.multiple_of(lax.rem(s, 8) * tall, 8)
            col = pl.multiple_of((s // 8) * half, 128)
            block = dn[pl.ds(start, tall), pl.ds(col, half)]
            for k in range(half // 256):
                unit = jnp.concatenate(
                    [block[:, 256 * k:256 * k + 128], block[:, 256 * k + 128:256 * (k + 1)]], axis=0
                )
                put(dy, dx, base + 2 * tall * k, unit)
    chips, toks, _ = keep_ref.shape
    mine = spot_ref[1]
    core = lax.rem(mine, 2)
    for k in range(chips):
        home = lax.rem(mine // 2 + k, chips) * 2
        for target, index in ((keep_ref, core), (give_ref, 1 - core)):
            at = pl.multiple_of((home + index) * toks, toks)
            target[k] = dot_nn(f_ref[pl.ds(at, toks), :], down_ref[...]).astype(BF16)


def ffn_grads(spot, place, n2, both, f, dgate, dup, down_mat, n_seq, n_f):
    rows, width = n2.shape
    own = f.shape[1]
    side = int(math.isqrt(n_seq))
    depth = n_f * UNITS * 16 + own * width // (n_seq * 128)
    piece = shape((side, depth // 2, 128), BF16)
    toks = rows // n_f
    outs = call(
        ffn_grads_kernel, "ffn_grads",
        [SMEM] * 2 + vmem(1) + [part_of((n_f, toks, width), 0, 1, 0)] + vmem(4),
        vmem(2 * side + 2),
        [piece] * (2 * side) + [shape((n_f // 2, toks, width), BF16)] * 2,
        [
            pltpu.VMEM((256, 640), F32),
            pltpu.VMEM((own, width), F32),
        ],
        8 * rows * width * own, 16 * 1024 * 1024,
        spot, place, n2, both, f, dgate, dup, down_mat,
    )
    return list(outs[:side]), list(outs[side:2 * side]), outs[2 * side], outs[2 * side + 1]


def mid_kernel(part_ref, h_ref, g_ref, gain_ref, mat_ref, dh1_ref, dh_ref, do_ref):
    incoming = part_ref[0].astype(F32)
    for c in range(1, part_ref.shape[0]):
        incoming = incoming + part_ref[c].astype(F32)
    h = h_ref[...]
    scale = lax.rsqrt(jnp.mean(h * h, axis=-1, keepdims=True) + EPS)
    dh1 = g_ref[...].astype(F32) + norm_back(h, scale, gain_ref[1:2, :], incoming)
    dh1_ref[...] = dh1
    dh = dh1.astype(BF16)
    dh_ref[...] = dh
    do = dot_nn(dh, mat_ref[...])
    for pair in range(do_ref.shape[0] // 2):
        early = do[0:HALF, pair * 128:(pair + 1) * 128]
        late = do[HALF:2 * HALF, pair * 128:(pair + 1) * 128]
        lane = lanes(early.shape)
        do_ref[2 * pair] = jnp.where(lane < HD, early, pltpu.roll(late, 64, 1)).astype(BF16)
        do_ref[2 * pair + 1] = jnp.where(lane < HD, pltpu.roll(early, 64, 1), late).astype(BF16)


def middle(parts, h1, g, gain, mat, heads):
    toks, width = h1.shape
    return call(
        mid_kernel, "middle", vmem(5), vmem(3),
        [
            shape((toks, width), F32),
            shape((toks, width), BF16),
            shape((heads, HALF, 128), BF16),
        ],
        [], 2 * toks * width * width, 6 * 1024 * 1024,
        parts, h1, g, gain, mat,
    )


def backward_kernel(
    where_ref, q_ref, k_ref, v_ref, kept_ref, do_ref, raw_ref, scale_ref, cos_ref, sin_ref,
    gain_ref, x_ref, chunk_ref,
    packed_ref, head_ref, dox, kt, dqt, dk_all, dv_all, grads,
):
    rows = q_ref.shape[0]
    count = rows // TILE
    half_blocks = rows // HALF // 2
    lane64 = lanes((HALF, 128))
    for block in range(2 * half_blocks):
        start = pl.multiple_of((where_ref[block] // 2) * HALF, HALF)
        do = do_ref[pl.ds(start, HALF), :].astype(F32)
        if block >= half_blocks:
            do = pltpu.roll(do, 64, 1)
        kept = kept_ref[block * HALF:(block + 1) * HALF, :]
        inverse = kept[:, HD:HD + 1]
        scaled = do * inverse
        delta = jnp.sum(jnp.where(lane64 < HD, scaled * kept, 0.0), axis=-1, keepdims=True)
        top = delta.astype(BF16).astype(F32)
        dox[block * HALF:(block + 1) * HALF, :] = jnp.where(
            lane64 < HD,
            scaled,
            jnp.where(lane64 == HD, -top, jnp.where(lane64 == HD + 1, top - delta, 0.0)),
        ).astype(BF16)
    for j in range(count):
        kt[:, j * TILE:(j + 1) * TILE] = k_ref[j * TILE:(j + 1) * TILE, :].astype(F32).T.astype(BF16)
    upper = lax.broadcasted_iota(jnp.int32, (TILE, TILE), 0) <= lax.broadcasted_iota(
        jnp.int32, (TILE, TILE), 1
    )
    for j in range(count):
        key = k_ref[j * TILE:(j + 1) * TILE, :]
        value = v_ref[j * TILE:(j + 1) * TILE, :]
        key_turned = kt[:, j * TILE:(j + 1) * TILE]
        dk = jnp.zeros((TILE, 128), F32)
        dv = jnp.zeros((TILE, 128), F32)
        for i in range(j, count):
            span = slice(i * TILE, (i + 1) * TILE)
            q = q_ref[span, :]
            do = dox[span, :]
            e = jnp.exp2(dot_nt(key, q))
            if i == j:
                e = jnp.where(upper, e, 0.0)
            ds = (e * dot_nt(value, do)).astype(BF16)
            dv = dv + dot_nn(e.astype(BF16), do)
            dk = dk + dot_nn(ds, q)
            part = dot_nn(key_turned, ds)
            if j == 0:
                dqt[:, span] = part
            else:
                dqt[:, span] += part
        dk_all[j * TILE:(j + 1) * TILE, :] = dk
        dv_all[j * TILE:(j + 1) * TILE, :] = dv
    lane = lanes((TILE, 128))
    gain = gain_ref[0:1, :]
    gain_sum = jnp.zeros((1, 128), F32)
    per = TILE // HALF
    for i in range(count):
        span = slice(i * TILE, (i + 1) * TILE)
        dq = dqt[:, span].T
        both = jnp.where(
            lane < HD, dq * (1.0 / math.sqrt(HD)), pltpu.roll(dk_all[span, :], 64, 1) * LN2
        )
        dz = both * cos_ref[span, :] - partner(both, lane) * sin_ref[span, :]
        raw = raw_ref[span, :]
        scale = lax.rsqrt(half_mean(raw * raw, lane) + EPS)
        u = dz * gain
        back = scale * u - raw * scale * scale * scale * half_mean(u * raw, lane)
        gain_sum = gain_sum + jnp.sum(dz * raw * scale, axis=0, keepdims=True)
        row_scale = scale_ref[span, :]
        dv = dv_all[span, :]
        back_scaled = (back * row_scale).astype(BF16)
        dv_scaled = jnp.where(lane < HD, dv * row_scale, 0.0).astype(BF16)
        back = back.astype(BF16)
        dv = dv[:, :HD].astype(BF16)
        for b in range(per):
            block = i * per + b
            sub = slice(b * HALF, (b + 1) * HALF)
            at = pl.multiple_of(where_ref[block] * HALF, HALF)
            grads[pl.ds(at, HALF), 0:128] = back_scaled[sub]
            grads[pl.ds(at, HALF), 128:256] = dv_scaled[sub]
            start = pl.multiple_of((where_ref[block] // 2) * HALF, HALF)
            if block < half_blocks:
                packed_ref[pl.ds(start, HALF), 0:128] = back[sub]
                packed_ref[pl.ds(start, HALF), 256:256 + HD] = dv[sub]
            else:
                packed_ref[pl.ds(start, HALF), 128:256] = back[sub]
                packed_ref[pl.ds(start, HALF), 256 + HD:384] = dv[sub]
    grad = grads[...]
    for c in range(head_ref.shape[0]):
        part = dot_tn(x_ref[:, c * 128:(c + 1) * 128], grad)
        head_ref[c, 0:128, :] = part[:, 0:128].astype(BF16)
        head_ref[c, 128:192, 0:HD] = part[0:HALF, 128:128 + HD].astype(BF16)
        head_ref[c, 128:192, HD:128] = part[HALF:128, 128:128 + HD].astype(BF16)
        head_ref[c, 192:208, :] = jnp.broadcast_to(gain_sum, (16, 128)).astype(BF16)
        head_ref[c, 208:336, :] = chunk_ref[c]


def attend_back(where, q, k, v, kept, do, raw, scale, cos, sin, gain, x_all, chunks):
    rows = q.shape[0]
    return call(
        backward_kernel, "attend_back", [SMEM] + vmem(12), vmem(2),
        [shape((rows // 2, 384), BF16), shape((chunks.shape[0], 336, 128), BF16)],
        [
            pltpu.VMEM((rows, 128), BF16),
            pltpu.VMEM((128, rows), BF16),
            pltpu.VMEM((128, rows), F32),
            pltpu.VMEM((rows, 128), F32),
            pltpu.VMEM((rows, 128), F32),
            pltpu.VMEM((rows, 256), BF16),
        ],
        6 * rows * rows * 128, 14 * 1024 * 1024,
        where, q, k, v, kept, do, raw, scale, cos, sin, gain, x_all, chunks,
    )


def tokens_kernel(in_ref, mat_ref, x_ref, dh1_ref, gain_ref, out_ref, wide):
    heads = in_ref.shape[0]
    kv_base = heads * HD
    v_base = kv_base + heads * HD // 2
    lane = lanes((HALF, 128))
    for half in range(2):
        rows = slice(half * HALF, (half + 1) * HALF)
        for pair in range(heads // 2):
            a = in_ref[2 * pair, :, half * 128:(half + 1) * 128].astype(F32)
            b = in_ref[2 * pair + 1, :, half * 128:(half + 1) * 128].astype(F32)
            wide[rows, pair * 128:(pair + 1) * 128] = jnp.where(
                lane < HD, a, pltpu.roll(b, 64, 1)
            ).astype(BF16)
        for quad in range(heads // 4):
            k = [in_ref[4 * quad + m, :, half * 128:(half + 1) * 128].astype(F32) for m in range(4)]
            v = [in_ref[4 * quad + m, :, 256:384].astype(F32) for m in range(4)]
            first_k, second_k = k[0] + k[1], k[2] + k[3]
            first_v, second_v = v[0] + v[1], v[2] + v[3]
            wide[rows, kv_base + quad * 128:kv_base + (quad + 1) * 128] = jnp.where(
                lane < HD, pltpu.roll(first_k, 64, 1), second_k
            ).astype(BF16)
            if half == 0:
                joined = jnp.where(lane < HD, first_v, pltpu.roll(second_v, 64, 1))
            else:
                joined = jnp.where(lane < HD, pltpu.roll(first_v, 64, 1), second_v)
            wide[rows, v_base + quad * 128:v_base + (quad + 1) * 128] = joined.astype(BF16)
    incoming = dot_nt(wide[...], mat_ref[...])
    x = x_ref[...].astype(F32)
    scale = lax.rsqrt(jnp.mean(x * x, axis=-1, keepdims=True) + EPS)
    out_ref[...] = (dh1_ref[...] + norm_back(x, scale, gain_ref[0:1, :], incoming)).astype(BF16)


def token_grads(arrived, mat, x, dh1, gain):
    toks, width = x.shape
    return call(
        tokens_kernel, "token_grads", vmem(5), vmem(1)[0],
        shape((toks, width), BF16),
        [pltpu.VMEM((toks, mat.shape[1]), BF16)],
        2 * toks * width * mat.shape[1], 6 * 1024 * 1024,
        arrived, mat, x, dh1, gain,
    )


def head_finish_kernel(
    in_ref, wq_ref, wk_ref, wv_ref, gain_ref, q_ref, k_ref, v_ref, out_ref, norm_ref, qk_ref
):
    heads = in_ref.shape[0]
    lane = lanes((128, 128))
    qk = jnp.zeros((16, 128), F32)
    for s in range(heads):
        qk = qk + in_ref[s, 192:208, :].astype(F32)
        for c in range(out_ref.shape[1] // 128):
            pair = in_ref[s, 208 + 8 * c - 8 * (c % 2):224 + 8 * c - 8 * (c % 2), :].astype(F32)
            out_ref[8 * s:8 * s + 8, c * 128:(c + 1) * 128] = pair[8 * (c % 2):8 * (c % 2) + 8]
    qk_ref[...] = qk[0:8]
    for pair in range(heads // 2):
        a = in_ref[2 * pair, 0:128, :].astype(F32)
        b = in_ref[2 * pair + 1, 0:128, :].astype(F32)
        q_ref[:, pair * 128:(pair + 1) * 128] = jnp.where(lane < HD, a, pltpu.roll(b, 64, 1))
    lane64 = lanes((HALF, 128))
    for quad in range(heads // 4):
        k = [in_ref[4 * quad + m, 0:128, :].astype(F32) for m in range(4)]
        v = [in_ref[4 * quad + m, 128:192, :].astype(F32) for m in range(4)]
        span = slice(quad * 128, (quad + 1) * 128)
        first_v, second_v = v[0] + v[1], v[2] + v[3]
        k_ref[:, span] = jnp.where(lane < HD, pltpu.roll(k[0] + k[1], 64, 1), k[2] + k[3])
        v_ref[0:HALF, span] = jnp.where(lane64 < HD, first_v, pltpu.roll(second_v, 64, 1))
        v_ref[HALF:128, span] = jnp.where(lane64 < HD, pltpu.roll(first_v, 64, 1), second_v)
    total = (
        jnp.sum(q_ref[...] * wq_ref[...].astype(F32), axis=1, keepdims=True)
        + jnp.sum(k_ref[...] * wk_ref[...].astype(F32), axis=1, keepdims=True)
        + jnp.sum(v_ref[...] * wv_ref[...].astype(F32), axis=1, keepdims=True)
    )
    norm_ref[...] = jnp.broadcast_to(total, (128, 128)).T[0:1]
    gain = jnp.broadcast_to(gain_ref[...], (128, 128)).T[:, 0:1]
    q_ref[...] = q_ref[...] * gain
    k_ref[...] = k_ref[...] * gain
    v_ref[...] = v_ref[...] * gain


def head_finish(last, wq, wk, wv, gain):
    own, width = wq.shape
    return call(
        head_finish_kernel, "head_finish", vmem(5), vmem(6),
        [
            shape(wq.shape, F32), shape(wk.shape, F32), shape(wv.shape, F32),
            shape((own, width), F32), shape((1, own), F32), shape((8, 128), F32),
        ],
        [], own * width * 4, 6 * 1024 * 1024,
        last, wq, wk, wv, gain,
    )


def ffn_finish_kernel(in_ref, wg_ref, wu_ref, gain_ref, gate_ref, up_ref, down_ref, norm_ref):
    n_seq, depth, _ = in_ref.shape
    ff = gate_ref.shape[1]
    own, width = down_ref.shape
    base = depth - own * width // (n_seq * 128)
    n_f = base // (UNITS * 16)
    tall = own // 8
    half = width // 2
    for s in range(n_seq):
        rows = slice(8 * s, 8 * s + 8)
        for c in range(n_f):
            for k in range(UNITS):
                lo = 128 * k
                hi = min(own, lo + 128)
                at = (c * UNITS + k) * 16
                unit = in_ref[s, at:at + 16, :].astype(F32)
                gate_ref[rows, c * own + lo:c * own + hi] = unit[0:8, 0:hi - lo]
                up_ref[rows, c * own + lo:c * own + hi] = unit[8:16, 0:hi - lo]
        start = tall * (s % 8)
        col = half * (s // 8)
        for k in range(half // 256):
            unit = in_ref[s, base + 2 * tall * k:base + 2 * tall * (k + 1), :].astype(F32)
            lo = col + 256 * k
            down_ref[start:start + tall, lo:lo + 128] = unit[:tall]
            down_ref[start:start + tall, lo + 128:lo + 256] = unit[tall:]
    total = jnp.sum(gate_ref[...] * wg_ref[...].astype(F32), axis=1, keepdims=True) + jnp.sum(
        up_ref[...] * wu_ref[...].astype(F32), axis=1, keepdims=True
    )
    norm_ref[...] = jnp.broadcast_to(total, (128, 128)).T[0:1] / gain_ref[...]


def ffn_finish(arrived, wg, wu, gain, down_shape):
    return call(
        ffn_finish_kernel, "ffn_finish", vmem(4), vmem(4),
        [
            shape(wg.shape, F32), shape(wu.shape, F32), shape(down_shape, F32),
            shape((1, wg.shape[0]), F32),
        ],
        [], wg.size * 4, 13 * 1024 * 1024,
        arrived, wg, wu, gain,
    )


def swap(a, axis):
    return lax.all_to_all(a, axis, split_axis=0, concat_axis=0, tiled=True)


def spread(a, axis):
    count = lax.axis_size(axis)
    return swap(jnp.broadcast_to(a[None], (count,) + a.shape), axis)


def gather(a, axis):
    return lax.all_gather(a, axis, axis=0, tiled=True)


def sum_parts(a):
    return jnp.sum(a.astype(F32), axis=0)


def after(value, *others):
    return lax.optimization_barrier((value,) + others)[0]


def norm_back(values, scaling, gain, incoming):
    weighted = incoming * gain
    inner = jnp.mean(weighted * values, axis=-1, keepdims=True)
    return scaling * weighted - values * scaling * scaling * scaling * inner


def along(step, is_x, side):
    if is_x:
        return [(i, (i // side) * side + (i % side + step) % side) for i in range(side * side)]
    return [(i, (i + side * step) % (side * side)) for i in range(side * side)]


def send_along(pieces, is_x):
    side = len(pieces)
    return [pieces[0]] + [
        lax.ppermute(pieces[step], "seq", along(step, is_x, side)) for step in range(1, side)
    ]


def add_up(pieces):
    total = pieces[0].astype(F32)
    for piece in pieces[1:]:
        total = total + piece.astype(F32)
    return total.astype(BF16)


def add_cores(keep, give, axis):
    got = lax.ppermute(give, axis, [(i, i ^ 1) for i in range(lax.axis_size(axis))])
    return (keep.astype(F32) + got.astype(F32)).astype(BF16)


def add_chips(pairs, axis):
    count = lax.axis_size(axis)
    total = pairs[0].astype(F32)
    for step in range(1, pairs.shape[0]):
        total = total + lax.ppermute(
            pairs[step], axis, [(i, (i + 2 * step) % count) for i in range(count)]
        ).astype(F32)
    return total


def body(
    tokens, cotangent, segments, pair_table, norm_gain, w_query, w_key, w_value,
    query_gain, key_gain, w_out, ffn_gain, w_gate, w_up, w_down,
):
    n_seq = lax.axis_size("seq")
    n_f = lax.axis_size("fsdp")
    me = lax.axis_index("seq")
    mine = lax.axis_index("fsdp")
    x_low = tokens[0]
    g_low = cotangent[0]
    toks, width = x_low.shape
    rows = toks * n_seq
    own_rows = w_query.shape[0]
    ff_own = w_gate.shape[1] // n_f
    gain_share = HD // n_f

    x_all = gather(x_low, "seq")

    slots = jnp.arange(n_seq, dtype=jnp.int32)
    slot_of = jnp.sum(
        jnp.where(pair_table[None, :] == slots[:, None], slots[None, :], 0), axis=1
    ).astype(jnp.int32)
    where = jnp.concatenate([2 * slot_of, 2 * slot_of[::-1] + 1])

    exponents = np.arange(0, HD, 2).astype(np.float32) / np.float32(HD)
    angles = np.arange(rows, dtype=np.float32)[:, None] * (
        np.float32(1.0) / np.float32(ROPE_BASE) ** exponents
    )[None, :]
    cosine = np.cos(angles).astype(np.float32)
    sine = np.sin(angles).astype(np.float32)
    cos = jnp.asarray(np.concatenate([cosine, cosine, cosine, cosine], axis=1))
    sin = jnp.asarray(np.concatenate([-sine, sine, -sine, sine], axis=1))
    doc = segments[0].astype(F32).reshape(-1, 128)

    spot = jnp.stack([me, mine]).astype(jnp.int32)
    gain_rows = jnp.pad(jnp.stack([norm_gain, ffn_gain]).astype(F32), ((0, 6), (0, 0)))
    w_parts, both = pack_weights(
        spot, query_gain.astype(F32), key_gain.astype(F32), gain_rows,
        w_query, w_key, w_value, w_gate, w_up, w_out, g_low, n_f,
    )
    w_big = swap(w_parts, "fsdp").reshape(width, -1)
    both_all = gather(both, "fsdp").reshape(n_f, -1, width)
    x_all, w_big, where = lax.optimization_barrier((x_all, w_big, where))

    o_packed, kept, raw, row_scale, q, k, v, gains, qk_gain = attend(
        where, x_all, w_big, cos, sin, doc
    )

    o_heads = swap(o_packed.reshape(n_seq, HALF, 128), "seq")
    h1, n2, o_chunks = project_out(o_heads, both_all, x_low, gains)
    n2_all = gather(n2, "fsdp")
    *mats, out_turned = prepare(after(w_big, n2), w_down, both_all)
    qkv_local = after(jnp.concatenate([w_query, w_key, w_value], axis=1), n2)
    qkv_mat = gather(qkv_local, "fsdp")

    dn2_part, f_low, dgate, dup = ffn(n2_all, both_all, mats)
    dn2_parts = swap(dn2_part, "fsdp")
    side = int(math.isqrt(n_seq))
    steps = jnp.arange(side, dtype=jnp.int32)
    place = (
        ((me // side + steps[:, None]) % side) * side + (me % side + steps[None, :]) % side
    ).reshape(n_seq)
    one, two, keep, give = ffn_grads(
        spot, place, n2_all, both_all, f_low, dgate, dup, w_down, n_seq, n_f
    )
    one = send_along(one, True)
    two = send_along(two[:-1] + [after(two[-1], one[1])], False)
    pairs = add_cores(keep, give, "fsdp")

    dn2_parts, one, two, qkv_mat = lax.optimization_barrier((dn2_parts, one, two, qkv_mat))
    dh1, dh, do = middle(dn2_parts, h1, g_low, gains, out_turned, n_seq)
    do_packed = swap(do, "seq").reshape(rows // 2, 128)
    do_packed, one, two = lax.optimization_barrier((do_packed, one, two))
    one, two = add_up(one), add_up(two)
    pack_sum = jnp.concatenate(
        [
            add_up(send_along([one[d] for d in range(side)], False)),
            add_up(send_along([two[d] for d in range(side)], True)),
        ],
        axis=0,
    )
    packed, head_part = attend_back(
        where, q, k, v, kept, do_packed, raw, row_scale, cos, sin, qk_gain, x_all, o_chunks
    )

    base = n_f * UNITS * 16
    pack_sum, packed = lax.optimization_barrier((pack_sum, packed))
    gu_rows = swap(pack_sum[:base].reshape(n_f, UNITS * 16, 128), "fsdp").reshape(base, 128)
    ffn_all = gather(jnp.concatenate([gu_rows, pack_sum[base:]], axis=0), "seq").reshape(
        n_seq, -1, 128
    )
    grad_gate, grad_up, grad_down, grad_ffn_gain = ffn_finish(
        ffn_all, w_gate, w_up, ffn_gain.astype(F32)[None], w_down.shape
    )

    dh_all = gather(dh, "fsdp")
    out_share = own_rows // n_seq
    head_all = swap(head_part, "fsdp")
    o_cols = head_all[:, 208:].reshape(n_f * toks, own_rows)
    out_part = dot_tn(o_cols, dh_all).astype(BF16)
    out_part = out_part.reshape(n_seq, out_share, width // 128, 128).transpose(0, 2, 1, 3)
    out_part = out_part.reshape(n_seq, HALF, 128)
    head_sum = sum_parts(head_all[:, :208])
    outgoing = jnp.concatenate([packed.reshape(n_seq, HALF, 384), out_part], axis=2)
    outgoing, pairs = lax.optimization_barrier((outgoing, pairs))
    arrived = swap(outgoing, "seq")
    block_out = (h1 + add_chips(pairs, "fsdp")).astype(BF16)
    out_sum = sum_parts(arrived[:, :, 384:])
    last = jnp.concatenate([head_sum, out_sum], axis=0).astype(BF16)
    last, block_out = lax.optimization_barrier((last, block_out))
    last = spread(last, "seq")
    grad_query, grad_key, grad_value, grad_out, grad_norm_gain, qk_sum = head_finish(
        last, w_query, w_key, w_value, norm_gain.astype(F32)[None]
    )
    grad_query_gain = lax.dynamic_slice_in_dim(qk_sum[0, :HD], mine * gain_share, gain_share)
    grad_key_gain = lax.dynamic_slice_in_dim(qk_sum[0, HD:], mine * gain_share, gain_share)

    grad_tokens = token_grads(arrived, qkv_mat, x_low, dh1, gains)

    return (
        block_out[None],
        grad_tokens[None],
        grad_norm_gain.reshape(own_rows),
        grad_query,
        grad_key,
        grad_value,
        grad_query_gain,
        grad_key_gain,
        grad_out,
        grad_ffn_gain.reshape(own_rows),
        grad_gate,
        grad_up,
        grad_down,
    )


def solution(mesh):
    row = P("fsdp", None)
    vec = P("fsdp")
    tok = P("fsdp", "seq", None)
    return jax.shard_map(
        body,
        mesh=mesh,
        in_specs=(
            tok, tok, row, P(), vec, row, row, row, vec, vec, row, vec, row, row, row,
        ),
        out_specs=(
            tok, tok, vec, row, row, row, vec, vec, row, vec, row, row, row,
        ),
        check_vma=False,
    )
```
